32 devices in a mesh: pool: 8 (over z, y), head: 4 (over x, core).
Axes of the slice: x: 2, y: 2, z: 4, core: 2. Of those that a mesh axis runs over, the one named last changes fastest.
Arguments:
- queries: bfloat16 [8, 2048, 8, 128], P('pool', None, 'head'), may hold values from -64 to 64
- new_pairs: bfloat16 [8, 2, 2048, 128], P('pool'), may hold values from -8 to 8
- kv_pool: bfloat16 [1024, 2, 64, 128], P('pool'), may hold values from -6 to 6
- page_owner: int32 [8, 64], P('pool'), may hold values from 0 to 7, as said below
- page_slot: int32 [8, 64], P('pool'), may hold values from 0 to 127, as said below
- prefix_len: int32 [8], P('pool'), may hold values from 2049 to 4096
- fresh_owner: int32 [8, 32], P('pool'), may hold values from 0 to 7, as said below
- fresh_slot: int32 [8, 32], P('pool'), may hold values from 0 to 31, as said below
Outputs:
- attended: bfloat16 [8, 2048, 8, 128], P('pool', None, 'head')
- stored: bfloat16 [256, 2, 64, 128], P('pool')
The draws below stay inside these ranges and needn't reach their ends.
Inputs may be any that keep to these rules, and one draw needn't show every extreme that they name: `page_owner`: for every request no owner holds more than 16 of the first ceil(prefix_len / 64) pages, and one owner, the same for all requests, holds exactly 16 of them for every request. `page_slot`: each (owner, slot) pair is named by at most one entry over all requests and all 64 entries. `fresh_owner`: for every request no owner receives more than 4 of its new pages, and one owner, the same for all requests, receives exactly 4 from every request. `fresh_slot`: each (owner, slot) pair is named by at most one new page over all requests.
All inputs are finite; a program needn't handle non-finite values.
Results may differ from the reference program's by a relative error of at most 0.0065.
Values may be sent and summed in bfloat16 or wider, within the bound.
A program may use at most 64 MiB of HBM per device.

```python
import math
import jax
import jax.numpy as jnp
from jax import lax

HD = 128
QHEADS = 8
PAGE = 64
NEW_TOK = 2048
MAXP = 64
REQS = 8
BUCKET = 16
SLOTS = 128
NEWP = 32
WB = 4
FRESH = 32
N_POOL = 8


def spread_cells(key, how_many, per_owner, front_len, salt):
    key = jax.random.fold_in(key, salt)
    four_keys = jax.random.split(key, 4)
    cell_total = N_POOL * per_owner
    crowded = jax.random.randint(four_keys[0], (), 0, N_POOL)
    indices = jnp.arange(cell_total, dtype=jnp.int32)
    scores = jax.random.randint(four_keys[1], (REQS, cell_total), 0, 1 << 20) * cell_total + indices[None, :] + cell_total
    scores = jnp.where((indices // per_owner)[None, :] == crowded, indices[None, :], scores)
    ordered = jnp.argsort(scores, axis=1)[:, :how_many].astype(jnp.int32)

    def shuffle_one(sub_key):
        return jax.random.permutation(sub_key, front_len)
    shuffles = jax.vmap(shuffle_one)(jax.random.split(four_keys[2], REQS)).astype(jnp.int32)
    head_part = jnp.take_along_axis(ordered[:, :front_len], shuffles, axis=1)
    ordered = jnp.concatenate([head_part, ordered[:, front_len:]], axis=1)
    owners = ordered // per_owner
    within = ordered % per_owner

    def slot_perm(sub_key):
        return jax.random.permutation(sub_key, REQS * per_owner)
    slot_table = jax.vmap(slot_perm)(jax.random.split(four_keys[3], N_POOL)).astype(jnp.int32)
    request_ids = jnp.arange(REQS, dtype=jnp.int32)[:, None]
    slot_ids = slot_table[owners, request_ids * per_owner + within]
    return (owners.astype(jnp.int32), slot_ids.astype(jnp.int32))


def draw_page_owner(key, part):
    shared = spread_cells(key, MAXP, BUCKET, MAXP // 2 + 1, 101)
    return shared[0]


def draw_page_slot(key, part):
    shared = spread_cells(key, MAXP, BUCKET, MAXP // 2 + 1, 101)
    return shared[1]


def draw_fresh_owner(key, part):
    shared = spread_cells(key, NEWP, WB, NEWP, 202)
    return shared[0]


def draw_fresh_slot(key, part):
    shared = spread_cells(key, NEWP, WB, NEWP, 202)
    return shared[1]


def draw_prefix_len(key, part):
    key = jax.random.fold_in(key, 51)
    first_key, second_key = jax.random.split(key, 2)
    top_len = MAXP * PAGE
    low_len = top_len // 2 + 1
    lengths = jax.random.randint(first_key, (REQS,), low_len, top_len + 1)
    order = jax.random.permutation(second_key, REQS)
    lengths = lengths.at[order[0]].set(top_len).at[order[1]].set(low_len)
    return lengths.astype(jnp.int32)


def draw_new_pairs(key, part):
    key = jax.random.fold_in(key, 31)
    key_key, value_key = jax.random.split(key, 2)
    key_rows = jnp.clip(jax.random.normal(key_key, (REQS, NEW_TOK, HD), jnp.float32), -6.0, 6.0)
    value_rows = jnp.clip(jax.random.normal(value_key, (REQS, NEW_TOK, HD), jnp.float32), -6.0, 6.0)
    return jnp.stack([key_rows, value_rows], axis=1).astype(jnp.bfloat16)


def draw_queries(key, part):
    key = jax.random.fold_in(key, 41)
    result = jnp.clip(jax.random.normal(key, (REQS, NEW_TOK, QHEADS, HD), jnp.float32), -6.0, 6.0)
    return result.astype(jnp.bfloat16)


def shard_levels(own_key, dims, pieces, smallest, high):
    def one(axis_at, shards_of):
        heights = jax.random.uniform(jax.random.fold_in(jax.random.fold_in(own_key, 6), axis_at), (shards_of,), jnp.float32, smallest / len(pieces), high / len(pieces))
        return jnp.repeat(jnp.exp(heights), dims[axis_at] // shards_of).reshape((-1,) + (1,) * (len(dims) - axis_at - 1))

    level = one(*pieces[0])
    for cut in pieces[1:]:
        level = level * one(*cut)
    return level


def normal_values(own_key, extent, scale, most, cuts=(), kind=jnp.bfloat16):
    values = scale * jax.random.normal(own_key, extent, jnp.float32)
    if cuts:
        values = values * shard_levels(own_key, extent, cuts, -0.22, 0.18)
    return jnp.clip(values, -most, most).astype(kind)


def setup_inputs(seed: int = 0) -> dict:
    arg_keys = jax.random.split(jax.random.key(seed), 9)
    return {
        "queries": draw_queries(jax.random.fold_in(arg_keys[8], 71), 0),
        "new_pairs": draw_new_pairs(jax.random.fold_in(arg_keys[8], 71), 0),
        "kv_pool": normal_values(arg_keys[2], (N_POOL * SLOTS, 2, PAGE, HD), 1.0, 6.0, ((0, 8),)),
        "page_owner": draw_page_owner(jax.random.fold_in(arg_keys[8], 71), 0),
        "page_slot": draw_page_slot(jax.random.fold_in(arg_keys[8], 71), 0),
        "prefix_len": draw_prefix_len(jax.random.fold_in(arg_keys[8], 71), 0),
        "fresh_owner": draw_fresh_owner(jax.random.fold_in(arg_keys[8], 71), 0),
        "fresh_slot": draw_fresh_slot(jax.random.fold_in(arg_keys[8], 71), 0),
    }


masked_score = -1e+30

def reference(queries, new_pairs, kv_pool, page_owner, page_slot, prefix_len, fresh_owner, fresh_slot):
    scaling = 1.0 / math.sqrt(HD)
    prefix_total = MAXP * PAGE
    key_pos = jnp.arange(prefix_total + NEW_TOK, dtype=jnp.int32)
    query_pos = jnp.arange(NEW_TOK, dtype=jnp.int32)

    def one_request(packed):
        query_rows, pair_rows, owners, slot_ids, length = packed
        pages_here = kv_pool[(owners * SLOTS + slot_ids).astype(jnp.int32)]
        key_rows = jnp.concatenate([pages_here[:, 0].reshape(-1, HD), pair_rows[0]], axis=0)
        value_rows = jnp.concatenate([pages_here[:, 1].reshape(-1, HD), pair_rows[1]], axis=0)
        allowed = jnp.where(key_pos[None, :] < prefix_total, key_pos[None, :] < length, key_pos[None, :] - prefix_total <= query_pos[:, None])

        def one_head(head_rows):
            scores = jnp.dot(head_rows, key_rows.T, preferred_element_type=jnp.float32) * scaling
            scores = jnp.where(allowed, scores, masked_score)
            weights = jnp.exp(scores - lax.optimization_barrier(jnp.max(scores, axis=1, keepdims=True)))
            totals = lax.optimization_barrier(jnp.sum(weights, axis=1))
            mixed = jnp.dot(weights.astype(jnp.bfloat16), value_rows, preferred_element_type=jnp.float32)
            return (mixed / totals[:, None]).astype(jnp.bfloat16)
        return jnp.transpose(lax.map(one_head, jnp.transpose(query_rows, (1, 0, 2))), (1, 0, 2))
    attended = lax.map(one_request, (queries, new_pairs, page_owner, page_slot, prefix_len))
    page_rows = new_pairs.reshape(REQS, 2, NEWP, PAGE, HD).transpose(0, 2, 1, 3, 4).reshape(REQS * NEWP, 2, PAGE, HD)
    targets = (fresh_owner * FRESH + fresh_slot).reshape(-1).astype(jnp.int32)
    stored = jnp.zeros((N_POOL * FRESH, 2, PAGE, HD), jnp.bfloat16).at[targets].set(page_rows)
    return (attended, stored)
```

```python
import functools
import math

import jax
import jax.numpy as jnp
from jax import lax
from jax.experimental import pallas as pl
from jax.experimental.pallas import tpu as pltpu
from jax.sharding import PartitionSpec as P

masked_score = -1e30


def place_cells(owners, slot_ids, is_live, per_owner, pool_count):
    how_many = owners.shape[0]
    indices = jnp.arange(how_many, dtype=jnp.int32)
    earlier = indices[:, None] > indices[None, :]
    same_owner = owners[:, None] == owners[None, :]
    position = jnp.sum(jnp.where(earlier & same_owner & is_live[None, :], 1, 0), axis=1).astype(
        jnp.int32
    )
    cell_ids = jnp.where(is_live, owners * per_owner + position, -1)
    matches = cell_ids[:, None] == jnp.arange(pool_count * per_owner, dtype=jnp.int32)[None, :]
    slot_table = jnp.sum(jnp.where(matches, slot_ids[:, None], 0), axis=0)
    return (cell_ids, matches, slot_table.reshape(pool_count, per_owner))


def absorb(q, k, v, m, acc, scale, keep=None):
    s = lax.dot_general(q, k, (((1,), (1,)), ((), ())), preferred_element_type=jnp.float32)
    if keep is not None:
        s = jnp.where(keep, s, masked_score)
    top = jnp.max(s, axis=1, keepdims=True)
    new_m = jnp.maximum(m, top)
    p = jnp.exp2((s - new_m[:, :1]) * scale).astype(jnp.bfloat16)
    fade = jnp.exp2((m - new_m) * scale)[:, :1]
    acc = acc * fade + jnp.dot(p, v, preferred_element_type=jnp.float32)
    return new_m, acc


def attend_kernel(
    len_ref, q_ref, new_ref, prefix_ref, out_ref, key_ref, value_ref, *, scale, block, heads, page_len, slice_len
):
    parts, _, part_len, dim = prefix_ref.shape
    new_len = new_ref.shape[1]
    rows = q_ref.shape[0]
    tokens = rows // heads
    prefix_total = parts * part_len
    step = pl.program_id(0)

    @pl.when(step == 0)
    def _():
        first = prefix_ref[0, 0, 0:16, :].astype(jnp.float32)[0:1, :]
        index = lax.broadcasted_iota(jnp.int32, (part_len, dim), 0)
        for part in range(parts):
            place = index // slice_len * page_len + part * slice_len + index % slice_len
            live = place < len_ref[0]
            rows_here = pl.ds(part * part_len, part_len)
            keys = prefix_ref[part, 0].astype(jnp.float32)
            key_ref[rows_here, :] = jnp.where(live, keys, first).astype(jnp.bfloat16)
            values = prefix_ref[part, 1].astype(jnp.float32)
            value_ref[rows_here, 0:dim] = jnp.where(live, values, 0.0).astype(jnp.bfloat16)
            value_ref[rows_here, dim:] = jnp.where(live, 1.0, 0.0).astype(jnp.bfloat16)
        value_ref[prefix_total:, 0:dim] = new_ref[1]
        value_ref[prefix_total:, dim:] = jnp.ones((new_len, dim), jnp.bfloat16)

    q = q_ref[...]
    m = jnp.full((rows, dim), masked_score, jnp.float32)
    acc = jnp.zeros((rows, 2 * dim), jnp.float32)

    def new_block(at, carry, keep=None):
        start = pl.multiple_of(at * block, block)
        k = new_ref[0, pl.ds(start, block), :]
        v = value_ref[pl.ds(prefix_total + start, block), :]
        return absorb(q, k, v, *carry, scale, keep)

    full = step * tokens // block
    row_token = step * tokens + lax.broadcasted_iota(jnp.int32, (rows, block), 0) // heads
    key_token = full * block + lax.broadcasted_iota(jnp.int32, (rows, block), 1)
    carry = new_block(full, (m, acc), key_token <= row_token)
    carry = lax.fori_loop(0, full, new_block, carry)
    for part in range(parts):
        here = pl.ds(part * part_len, part_len)
        carry = absorb(q, key_ref[here, :], value_ref[here, :], *carry, scale)
    acc = carry[1]
    out_ref[...] = (acc[:, :dim] / acc[:, dim:]).astype(out_ref.dtype)


def attend(q, new_pairs, prefix, length, page_len, slice_len, heads):
    rows, dim = q.shape
    new_len = new_pairs.shape[1]
    row_block = math.gcd(rows, 512)
    block = math.gcd(new_len, 512)
    parts, _, part_len, _ = prefix.shape
    kernel = functools.partial(
        attend_kernel,
        scale=math.log2(math.e) / math.sqrt(dim),
        block=block,
        heads=heads,
        page_len=page_len,
        slice_len=slice_len,
    )
    return pl.pallas_call(
        kernel,
        out_shape=jax.ShapeDtypeStruct((rows, dim), jnp.bfloat16),
        grid=(rows // row_block,),
        in_specs=[
            pl.BlockSpec(memory_space=pltpu.SMEM),
            pl.BlockSpec((row_block, dim), lambda i: (i, 0)),
            pl.BlockSpec(new_pairs.shape, lambda i: (0, 0, 0)),
            pl.BlockSpec(prefix.shape, lambda i: (0, 0, 0, 0)),
        ],
        out_specs=pl.BlockSpec((row_block, dim), lambda i: (i, 0)),
        scratch_shapes=[
            pltpu.VMEM((parts * part_len, dim), jnp.bfloat16),
            pltpu.VMEM((parts * part_len + new_len, 2 * dim), jnp.bfloat16),
        ],
        compiler_params=pltpu.CompilerParams(vmem_limit_bytes=48 * 1024 * 1024),
    )(length, q, new_pairs, prefix)


def exchange(x):
    return lax.all_to_all(x, "pool", split_axis=0, concat_axis=0, tiled=True)


def shards(queries, new_pairs, kv_pool, page_owner, page_slot, prefix_len, fresh_owner, fresh_slot):
    pool_count = lax.axis_size("pool")
    head_count = lax.axis_size("head")
    me_head = lax.axis_index("head")
    page_len = kv_pool.shape[2]
    dim = kv_pool.shape[3]
    slice_len = page_len // head_count
    max_pages = page_owner.shape[1]
    bucket = 2 * ((max_pages + pool_count - 1) // pool_count)
    new_len = new_pairs.shape[2]
    new_count = new_len // page_len
    write_bound = (new_count + pool_count - 1) // pool_count
    fresh_total = pool_count * write_bound
    length = prefix_len[0]

    live_pages = (length + page_len - 1) // page_len
    is_live = jnp.arange(max_pages, dtype=jnp.int32) < live_pages
    prefix_cells, _, request_table = place_cells(
        page_owner[0], page_slot[0], is_live, bucket, pool_count
    )
    fresh_cells, fresh_matches, dest_table = place_cells(
        fresh_owner[0],
        fresh_slot[0],
        jnp.ones((new_count,), dtype=bool),
        write_bound,
        pool_count,
    )
    filled = jnp.any(fresh_matches, axis=0).reshape(pool_count, write_bound)
    dest_slots = jnp.where(filled, dest_table, fresh_total)
    source = jnp.sum(
        jnp.where(fresh_matches, jnp.arange(new_count, dtype=jnp.int32)[:, None], 0), axis=0
    )
    tables = exchange(jnp.concatenate([request_table, dest_slots], axis=1))
    wanted, arrived_slots = tables[:, :bucket], tables[:, bucket:]

    pool_slice = lax.dynamic_slice_in_dim(kv_pool, me_head * slice_len, slice_len, 2)
    fetched = exchange(pool_slice[wanted]).reshape(pool_count * bucket, 2, slice_len, dim)
    mine = jnp.take(fetched, jnp.maximum(prefix_cells, 0), axis=0)
    mine = mine.transpose(1, 0, 2, 3).reshape(2, max_pages * slice_len, dim)
    prefix = lax.all_gather(mine, "head")

    new_pages = new_pairs[0].reshape(2, new_count, page_len, dim)
    new_slice = lax.dynamic_slice_in_dim(new_pages, me_head * slice_len, slice_len, 2)
    outgoing = jnp.take(new_slice.transpose(1, 0, 2, 3), source, axis=0)
    arrived = exchange(outgoing.reshape(pool_count, write_bound, 2, slice_len, dim))
    arrived = arrived.reshape(-1, 2, slice_len, dim)
    own = jnp.zeros((fresh_total, 2, slice_len, dim), jnp.bfloat16)
    own = own.at[arrived_slots.reshape(-1)].set(arrived, mode="drop")
    stored = lax.all_gather(own, "head")
    stored = stored.transpose(1, 2, 0, 3, 4).reshape(fresh_total, 2, page_len, dim)

    heads = queries.shape[2]
    attended = attend(
        queries.reshape(-1, dim), new_pairs[0], prefix, prefix_len, page_len, slice_len, heads
    )
    return (attended.reshape(queries.shape), stored)


def solution(mesh):
    in_specs = (
        P("pool", None, "head", None),
        P("pool", None, None, None),
        P("pool", None, None, None),
        P("pool", None),
        P("pool", None),
        P("pool"),
        P("pool", None),
        P("pool", None),
    )
    out_specs = (P("pool", None, "head", None), P("pool", None, None, None))
    return jax.shard_map(shards, mesh=mesh, in_specs=in_specs, out_specs=out_specs, check_vma=False)
```

```python
import functools
import math

import jax
import jax.numpy as jnp
from jax import lax
from jax.experimental import pallas as pl
from jax.experimental.pallas import tpu as pltpu
from jax.sharding import PartitionSpec as P

masked_score = -1e30
MESH = pl.DeviceIdType.MESH


def place_cells(owners, slot_ids, is_live, per_owner, pool_count):
    how_many = owners.shape[0]
    indices = jnp.arange(how_many, dtype=jnp.int32)
    earlier = indices[:, None] > indices[None, :]
    same_owner = owners[:, None] == owners[None, :]
    position = jnp.sum(jnp.where(earlier & same_owner & is_live[None, :], 1, 0), axis=1).astype(
        jnp.int32
    )
    cell_ids = jnp.where(is_live, owners * per_owner + position, -1)
    matches = cell_ids[:, None] == jnp.arange(pool_count * per_owner, dtype=jnp.int32)[None, :]
    slot_table = jnp.sum(jnp.where(matches, slot_ids[:, None], 0), axis=0)
    return (cell_ids, matches, slot_table.reshape(pool_count, per_owner))


def absorb(q, k, v, m, acc, scale, keep=None):
    s = lax.dot_general(q, k, (((1,), (1,)), ((), ())), preferred_element_type=jnp.float32)
    if keep is not None:
        s = jnp.where(keep, s, masked_score)
    top = jnp.max(s, axis=1, keepdims=True)
    new_m = jnp.maximum(m, top)
    p = jnp.exp2((s - new_m[:, :1]) * scale).astype(jnp.bfloat16)
    fade = jnp.exp2((m - new_m) * scale)[:, :1]
    acc = acc * fade + jnp.dot(p, v, preferred_element_type=jnp.float32)
    return new_m, acc


def fused_kernel(
    len_ref,
    cell_ref,
    source_ref,
    table_ref,
    q_ref,
    new_ref,
    pool_ref,
    out_ref,
    stored_ref,
    slice_ref,
    asked_ref,
    asked_smem,
    place_ref,
    place_smem,
    page_out,
    key_in,
    value_in,
    fresh_out,
    fresh_in,
    part_ref,
    value_ref,
    new_value_ref,
    m_ref,
    acc_ref,
    load_sem,
    small_sem,
    table_send,
    table_recv,
    fresh_send,
    fresh_recv,
    page_send,
    page_recv,
    part_send,
    part_recv,
    stored_send,
    stored_recv,
    *,
    scale,
    row_block,
    heads,
):
    pools, _, bucket, piece, dim = page_out.shape[1], 2, page_out.shape[2], page_out.shape[3], page_out.shape[4]
    head_count = part_ref.shape[0]
    part_len = part_ref.shape[2]
    bound = fresh_out.shape[1]
    slots = stored_ref.shape[0]
    page_len = stored_ref.shape[2]
    max_pages = cell_ref.shape[0]
    new_pages = new_ref.shape[1]
    page_in = (key_in, value_in)
    me = lax.axis_index("pool")
    side = lax.axis_index("head")
    mine = pl.ds(pl.multiple_of(side * piece, piece), piece)
    by_pair = side + 1 - 2 * (side % 2)
    half = head_count // 2
    across = (side + half) % head_count

    load = pltpu.make_async_copy(pool_ref.at[:, :, mine, :], slice_ref, load_sem)
    load.start()

    barrier = pltpu.get_barrier_semaphore()

    def greet(d, carry):
        pl.semaphore_signal(barrier, inc=1, device_id={"pool": (me + d) % pools}, device_id_type=MESH)
        return carry

    lax.fori_loop(1, pools, greet, 0)
    for peer in (by_pair, across):
        pl.semaphore_signal(barrier, inc=1, device_id={"head": peer}, device_id_type=MESH)
    pl.semaphore_wait(barrier, pools - 1 + 2)

    def remote(src, dst, send, recv, axis, peer):
        return pltpu.make_async_remote_copy(
            src_ref=src,
            dst_ref=dst,
            send_sem=send,
            recv_sem=recv,
            device_id={axis: peer},
            device_id_type=MESH,
        )

    def table_copy(d):
        to = (me + d) % pools
        return remote(table_ref.at[to], asked_ref.at[me], table_send.at[d], table_recv.at[d], "pool", to)

    def fresh_copy(d):
        to = (me + d) % pools
        return remote(fresh_out.at[to], fresh_in.at[me], fresh_send.at[d], fresh_recv.at[d], "pool", to)

    def page_copy(kv, d):
        to = (me + d) % pools
        return remote(
            page_out.at[kv, to], page_in[kv].at[me], page_send.at[kv, d], page_recv.at[kv, d], "pool", to
        )

    def each(start, stop, act):
        def body(d, carry):
            act(d)
            return carry

        lax.fori_loop(start, stop, body, 0)

    each(1, pools, lambda d: table_copy(d).start())
    asked_ref[me] = table_ref[me]
    load.wait()
    each(1, pools, lambda d: table_copy(d).wait())
    total = asked_ref[0, 1:2, :]
    for r in range(1, pools):
        total = total + asked_ref[r, 1:2, :]
    place_ref[...] = total
    to_smem = pltpu.make_async_copy(asked_ref, asked_smem, small_sem.at[0])
    to_smem.start()
    place_copy = pltpu.make_async_copy(place_ref, place_smem, small_sem.at[1])
    place_copy.start()
    to_smem.wait()
    place_copy.wait()

    def pages_to(kv, d):
        to = (me + d) % pools
        for c in range(bucket):
            page_out[kv, to, c] = slice_ref[asked_smem[to, 0, c], kv]

    for kv in range(2):

        def send_pages(d):
            pages_to(kv, d)
            page_copy(kv, d).start()

        each(1, pools, send_pages)
        pages_to(kv, 0)
        page_in[kv][me] = page_out[kv, me]

    def fresh_to(d):
        to = (me + d) % pools
        for c in range(bound):
            page = source_ref[to * bound + c]
            for kv in range(2):
                fresh_out[to, c, kv] = new_ref[kv, page, mine, :]

    def send_fresh(d):
        fresh_to(d)
        fresh_copy(d).start()

    each(1, pools, send_fresh)
    fresh_to(0)
    fresh_in[me] = fresh_out[me]

    new_value_ref[:, 0:dim] = new_ref[1].reshape(new_pages * page_len, dim)
    new_value_ref[:, dim:] = jnp.ones((new_pages * page_len, dim), jnp.bfloat16)
    tokens = row_block // heads
    row_blocks = q_ref.shape[0] // row_block

    def new_rows(i):
        rows = pl.ds(pl.multiple_of(i * row_block, row_block), row_block)
        q = q_ref[rows, :]
        m = jnp.full((row_block, dim), masked_score, jnp.float32)
        acc = jnp.zeros((row_block, 2 * dim), jnp.float32)

        def new_block(at, carry, keep=None):
            k = new_ref[0, pl.ds(at * (tokens // page_len), tokens // page_len)].reshape(tokens, dim)
            v = new_value_ref[pl.ds(pl.multiple_of(at * tokens, tokens), tokens), :]
            return absorb(q, k, v, *carry, scale, keep)

        row_token = lax.broadcasted_iota(jnp.int32, (row_block, tokens), 0) // heads
        keep = lax.broadcasted_iota(jnp.int32, (row_block, tokens), 1) <= row_token
        m, acc = lax.fori_loop(0, i, new_block, new_block(i, (m, acc), keep))
        m_ref[rows, :] = m
        acc_ref[rows, :] = acc

    def part_copy(kv, which):
        part, peer = ((side, across), (side, by_pair), (across, by_pair))[which]
        return remote(
            part_ref.at[part, kv],
            part_ref.at[part, kv],
            part_send.at[kv, which],
            part_recv.at[kv, which],
            "head",
            peer,
        )

    def collect(kv):
        each(1, pools, lambda d: page_copy(kv, d).wait())

        def four(g, carry):
            for j in range(4):
                cell = cell_ref[g * 4 + j]
                rows = pl.ds(pl.multiple_of((g * 4 + j) * piece, piece), piece)
                part_ref[side, kv, rows, :] = page_in[kv][cell // bucket, cell % bucket]
            return carry

        lax.fori_loop(0, max_pages // 4, four, 0)
        part_copy(kv, 0).start()
        part_copy(kv, 1).start()

    each(0, row_blocks * 5 // 8, new_rows)
    collect(0)
    each(row_blocks * 5 // 8, row_blocks, new_rows)
    part_copy(0, 0).wait()
    part_copy(0, 2).start()
    collect(1)

    each(1, pools, lambda d: fresh_copy(d).wait())

    def keep_page(s):
        at = place_smem[0, s]
        cell = jnp.maximum(at - 1, 0)
        filled = jnp.full((piece, dim), at, jnp.int32) > 0
        for kv in range(2):
            page = fresh_in[cell // bound, cell % bound, kv].astype(jnp.float32)
            stored_ref[s, kv, mine, :] = jnp.where(filled, page, 0.0).astype(jnp.bfloat16)

    each(0, slots, keep_page)

    def stored_copy(which):
        part, peer = ((side, across), (side, by_pair), (across, by_pair))[which]
        rows = stored_ref.at[:, :, pl.ds(pl.multiple_of(part * piece, piece), piece), :]
        return remote(rows, rows, stored_send.at[which], stored_recv.at[which], "head", peer)

    stored_copy(0).start()
    stored_copy(1).start()
    part_copy(1, 0).wait()
    part_copy(1, 2).start()
    stored_copy(0).wait()
    stored_copy(2).start()
    for which in (1, 2):
        part_copy(0, which).wait()
        part_copy(1, which).wait()

    def stored_wait():
        stored_copy(1).wait()
        stored_copy(2).wait()

    first = part_ref[0, 0, 0:16, :].astype(jnp.float32)[0:1, :]
    index = lax.broadcasted_iota(jnp.int32, (part_len, dim), 0)
    for part in range(head_count):
        place = index // piece * page_len + part * piece + index % piece
        live = place < len_ref[0]
        keys = part_ref[part, 0].astype(jnp.float32)
        part_ref[part, 0] = jnp.where(live, keys, first).astype(jnp.bfloat16)
        values = part_ref[part, 1].astype(jnp.float32)
        value_ref[part, :, 0:dim] = jnp.where(live, values, 0.0).astype(jnp.bfloat16)
        value_ref[part, :, dim:] = jnp.where(live, 1.0, 0.0).astype(jnp.bfloat16)

    def prefix_rows(i):
        rows = pl.ds(pl.multiple_of(i * row_block, row_block), row_block)
        q = q_ref[rows, :]
        carry = (m_ref[rows, :], acc_ref[rows, :])
        for part in range(head_count):
            carry = absorb(q, part_ref[part, 0], value_ref[part], *carry, scale)
        acc = carry[1]
        out_ref[rows, :] = (acc[:, :dim] / acc[:, dim:]).astype(out_ref.dtype)

    each(0, row_blocks, prefix_rows)
    stored_wait()


def fused(q, new_pairs, kv_pool, table, cells, source, length, slots, bucket, bound, pools, head_count, heads):
    rows, dim = q.shape
    new_pages, page_len = new_pairs.shape[1:3]
    piece = page_len // head_count
    max_pages = cells.shape[0]
    row_block = math.gcd(rows, 512)
    kernel = functools.partial(
        fused_kernel,
        scale=math.log2(math.e) / math.sqrt(dim),
        row_block=row_block,
        heads=heads,
    )
    bf16, dma = jnp.bfloat16, pltpu.SemaphoreType.DMA
    smem, vmem = pl.BlockSpec(memory_space=pltpu.SMEM), pl.BlockSpec(memory_space=pltpu.VMEM)
    part_len = max_pages * piece
    return pl.pallas_call(
        kernel,
        out_shape=(
            jax.ShapeDtypeStruct((rows, dim), bf16),
            jax.ShapeDtypeStruct((slots, 2, page_len, dim), bf16),
        ),
        in_specs=[smem, smem, smem, vmem, vmem, vmem, pl.BlockSpec(memory_space=pl.ANY)],
        out_specs=(vmem, vmem),
        scratch_shapes=[
            pltpu.VMEM((kv_pool.shape[0], 2, piece, dim), bf16),
            pltpu.VMEM(table.shape, jnp.int32),
            pltpu.SMEM(table.shape, jnp.int32),
            pltpu.VMEM((1, 128), jnp.int32),
            pltpu.SMEM((1, 128), jnp.int32),
            pltpu.VMEM((2, pools, bucket, piece, dim), bf16),
            pltpu.VMEM((pools, bucket, piece, dim), bf16),
            pltpu.VMEM((pools, bucket, piece, dim), bf16),
            pltpu.VMEM((pools, bound, 2, piece, dim), bf16),
            pltpu.VMEM((pools, bound, 2, piece, dim), bf16),
            pltpu.VMEM((head_count, 2, part_len, dim), bf16),
            pltpu.VMEM((head_count, part_len, 2 * dim), bf16),
            pltpu.VMEM((new_pages * page_len, 2 * dim), bf16),
            pltpu.VMEM((rows, dim), jnp.float32),
            pltpu.VMEM((rows, 2 * dim), jnp.float32),
            dma,
            dma((2,)),
            dma((pools,)),
            dma((pools,)),
            dma((pools,)),
            dma((pools,)),
            dma((2, pools)),
            dma((2, pools)),
            dma((2, 3)),
            dma((2, 3)),
            dma((3,)),
            dma((3,)),
        ],
        compiler_params=pltpu.CompilerParams(
            vmem_limit_bytes=56 * 1024 * 1024, collective_id=0, has_side_effects=True
        ),
    )(length, cells, source, table, q, new_pairs, kv_pool)


def shards(queries, new_pairs, kv_pool, page_owner, page_slot, prefix_len, fresh_owner, fresh_slot):
    pool_count = lax.axis_size("pool")
    head_count = lax.axis_size("head")
    page_len = kv_pool.shape[2]
    dim = kv_pool.shape[3]
    max_pages = page_owner.shape[1]
    bucket = 2 * ((max_pages + pool_count - 1) // pool_count)
    new_len = new_pairs.shape[2]
    new_count = new_len // page_len
    write_bound = (new_count + pool_count - 1) // pool_count
    fresh_total = pool_count * write_bound
    length = prefix_len[0]

    live_pages = (length + page_len - 1) // page_len
    is_live = jnp.arange(max_pages, dtype=jnp.int32) < live_pages
    prefix_cells, _, request_table = place_cells(
        page_owner[0], page_slot[0], is_live, bucket, pool_count
    )
    fresh_cells, fresh_matches, _ = place_cells(
        fresh_owner[0],
        fresh_slot[0],
        jnp.ones((new_count,), dtype=bool),
        write_bound,
        pool_count,
    )
    source = jnp.sum(
        jnp.where(fresh_matches, jnp.arange(new_count, dtype=jnp.int32)[:, None], 0), axis=0
    )
    rank = fresh_cells % write_bound + lax.axis_index("pool") * write_bound + 1
    spot = fresh_owner[0] * 128 + fresh_slot[0]
    lanes = jnp.arange(pool_count * 128, dtype=jnp.int32)
    places = jnp.sum(jnp.where(spot[:, None] == lanes[None, :], rank[:, None], 0), axis=0)
    table = jnp.stack(
        [jnp.pad(request_table, ((0, 0), (0, 128 - bucket))), places.reshape(pool_count, 128)], axis=1
    )

    heads = queries.shape[2]
    attended, stored = fused(
        queries.reshape(-1, dim),
        new_pairs[0].reshape(2, new_count, page_len, dim),
        kv_pool,
        table,
        jnp.maximum(prefix_cells, 0),
        source,
        prefix_len,
        fresh_total,
        bucket,
        write_bound,
        pool_count,
        head_count,
        heads,
    )
    return (attended.reshape(queries.shape), stored)


def solution(mesh):
    in_specs = (
        P("pool", None, "head", None),
        P("pool", None, None, None),
        P("pool", None, None, None),
        P("pool", None),
        P("pool", None),
        P("pool"),
        P("pool", None),
        P("pool", None),
    )
    out_specs = (P("pool", None, "head", None), P("pool", None, None, None))
    return jax.shard_map(shards, mesh=mesh, in_specs=in_specs, out_specs=out_specs, check_vma=False)
```

```python
import functools
import math

import jax
import jax.numpy as jnp
from jax import lax
from jax.experimental import pallas as pl
from jax.experimental.pallas import tpu as pltpu
from jax.sharding import PartitionSpec as P

masked_score = -1e30
MESH = pl.DeviceIdType.MESH


def place_cells(owners, slot_ids, is_live, per_owner, pool_count):
    how_many = owners.shape[0]
    indices = jnp.arange(how_many, dtype=jnp.int32)
    earlier = indices[:, None] > indices[None, :]
    same_owner = owners[:, None] == owners[None, :]
    position = jnp.sum(jnp.where(earlier & same_owner & is_live[None, :], 1, 0), axis=1).astype(
        jnp.int32
    )
    cell_ids = jnp.where(is_live, owners * per_owner + position, -1)
    matches = cell_ids[:, None] == jnp.arange(pool_count * per_owner, dtype=jnp.int32)[None, :]
    slot_table = jnp.sum(jnp.where(matches, slot_ids[:, None], 0), axis=0)
    return (cell_ids, matches, slot_table.reshape(pool_count, per_owner))


def absorb(q, k, v, m, acc, scale, keep=None):
    s = lax.dot_general(q, k, (((1,), (1,)), ((), ())), preferred_element_type=jnp.float32)
    if keep is not None:
        s = jnp.where(keep, s, masked_score)
    return weigh(s, v, m, acc, scale)


def weigh(s, v, m, acc, scale):
    top = jnp.max(s, axis=1, keepdims=True)
    new_m = jnp.maximum(m, top)
    p = jnp.exp2((s - new_m[:, :1]) * scale).astype(jnp.bfloat16)
    fade = jnp.exp2((m - new_m) * scale)[:, :1]
    acc = acc * fade + jnp.dot(p, v, preferred_element_type=jnp.float32)
    return new_m, acc


def fused_kernel(
    len_ref,
    cell_ref,
    source_ref,
    table_ref,
    q_ref,
    new_ref,
    pool_ref,
    out_ref,
    stored_ref,
    slice_ref,
    asked_ref,
    asked_smem,
    place_ref,
    place_smem,
    page_out,
    first_in,
    second_in,
    fresh_out,
    fresh_in,
    part_ref,
    value_ref,
    new_value_ref,
    m_ref,
    acc_ref,
    load_sem,
    small_sem,
    table_send,
    table_recv,
    fresh_send,
    fresh_recv,
    page_send,
    page_recv,
    part_send,
    part_recv,
    stored_send,
    stored_recv,
    *,
    scale,
    row_block,
    heads,
):
    _, pools, bucket, _, piece, dim = page_out.shape
    part_len = cell_ref.shape[0] // 2 * piece
    head_count = part_ref.shape[2] // part_len
    bound = fresh_out.shape[1]
    slots = stored_ref.shape[0]
    page_len = stored_ref.shape[2]
    max_pages = cell_ref.shape[0]
    new_pages = new_ref.shape[1]
    page_in = (first_in, second_in)
    me = lax.axis_index("pool")
    side = lax.axis_index("head")
    mine = pl.ds(pl.multiple_of(side * piece, piece), piece)
    by_pair = side + 1 - 2 * (side % 2)
    half = head_count // 2
    across = (side + half) % head_count

    load = pltpu.make_async_copy(pool_ref.at[:, :, mine, :], slice_ref, load_sem)
    load.start()

    barrier = pltpu.get_barrier_semaphore()

    def greet(d, carry):
        pl.semaphore_signal(barrier, inc=1, device_id={"pool": (me + d) % pools}, device_id_type=MESH)
        return carry

    lax.fori_loop(1, pools, greet, 0)
    for peer in (by_pair, across):
        pl.semaphore_signal(barrier, inc=1, device_id={"head": peer}, device_id_type=MESH)
    pl.semaphore_wait(barrier, pools - 1 + 2)

    def remote(src, dst, send, recv, axis, peer):
        return pltpu.make_async_remote_copy(
            src_ref=src,
            dst_ref=dst,
            send_sem=send,
            recv_sem=recv,
            device_id={axis: peer},
            device_id_type=MESH,
        )

    def table_copy(d):
        to = (me + d) % pools
        return remote(table_ref.at[to], asked_ref.at[me], table_send.at[d], table_recv.at[d], "pool", to)

    def fresh_copy(d):
        to = (me + d) % pools
        return remote(fresh_out.at[to], fresh_in.at[me], fresh_send.at[d], fresh_recv.at[d], "pool", to)

    def page_copy(kv, d):
        to = (me + d) % pools
        return remote(
            page_out.at[kv, to], page_in[kv].at[me], page_send.at[kv, d], page_recv.at[kv, d], "pool", to
        )

    def each(start, stop, act):
        def body(d, carry):
            act(d)
            return carry

        lax.fori_loop(start, stop, body, 0)

    each(1, pools, lambda d: table_copy(d).start())
    asked_ref[me] = table_ref[me]
    load.wait()
    each(1, pools, lambda d: table_copy(d).wait())
    total = asked_ref[0, 1:2, :]
    for r in range(1, pools):
        total = total + asked_ref[r, 1:2, :]
    place_ref[...] = total
    to_smem = pltpu.make_async_copy(asked_ref, asked_smem, small_sem.at[0])
    to_smem.start()
    place_copy = pltpu.make_async_copy(place_ref, place_smem, small_sem.at[1])
    place_copy.start()
    to_smem.wait()
    place_copy.wait()

    def pages_to(part, d):
        to = (me + d) % pools
        for c in range(bucket):
            page_out[part, to, c] = slice_ref[asked_smem[to, 0, part * bucket + c]]

    for part in range(2):

        def send_pages(d):
            pages_to(part, d)
            page_copy(part, d).start()

        each(1, pools, send_pages)
        pages_to(part, 0)
        page_in[part][me] = page_out[part, me]

    def fresh_to(d):
        to = (me + d) % pools
        for c in range(bound):
            page = source_ref[to * bound + c]
            for kv in range(2):
                fresh_out[to, c, kv] = new_ref[kv, page, mine, :]

    def send_fresh(d):
        fresh_to(d)
        fresh_copy(d).start()

    each(1, pools, send_fresh)
    fresh_to(0)
    fresh_in[me] = fresh_out[me]

    new_value_ref[:, 0:dim] = new_ref[1].reshape(new_pages * page_len, dim)
    new_value_ref[:, dim:] = jnp.ones((new_pages * page_len, dim), jnp.bfloat16)
    tokens = row_block // heads
    row_blocks = q_ref.shape[0] // row_block

    def new_rows(i):
        rows = pl.ds(pl.multiple_of(i * row_block, row_block), row_block)
        q = q_ref[rows, :]
        m = jnp.full((row_block, dim), masked_score, jnp.float32)
        acc = jnp.zeros((row_block, 2 * dim), jnp.float32)

        def new_block(at, carry, keep=None):
            k = new_ref[0, pl.ds(at * (tokens // page_len), tokens // page_len)].reshape(tokens, dim)
            v = new_value_ref[pl.ds(pl.multiple_of(at * tokens, tokens), tokens), :]
            return absorb(q, k, v, *carry, scale, keep)

        row_token = lax.broadcasted_iota(jnp.int32, (row_block, tokens), 0) // heads
        keep = lax.broadcasted_iota(jnp.int32, (row_block, tokens), 1) <= row_token
        m, acc = lax.fori_loop(0, i, new_block, new_block(i, (m, acc), keep))
        m_ref[rows, :] = m
        acc_ref[rows, :] = acc

    def part_rows(part):
        return pl.ds(pl.multiple_of(part * part_len, part_len), part_len)

    def part_copy(half_at, which):
        part, peer = ((side, across), (side, by_pair), (across, by_pair))[which]
        return remote(
            part_ref.at[half_at, :, part_rows(part), :],
            part_ref.at[half_at, :, part_rows(part), :],
            part_send.at[half_at, which],
            part_recv.at[half_at, which],
            "head",
            peer,
        )

    def collect(half_at):
        each(1, pools, lambda d: page_copy(half_at, d).wait())
        count = part_len // piece

        def four(g):
            for j in range(4):
                cell = cell_ref[half_at * count + g * 4 + j]
                rows = pl.ds(pl.multiple_of(side * part_len + (g * 4 + j) * piece, piece), piece)
                for kv in range(2):
                    part_ref[half_at, kv, rows, :] = page_in[half_at][cell // bucket, cell % bucket, kv]

        each(0, count // 4, four)
        part_copy(half_at, 0).start()
        part_copy(half_at, 1).start()

    live_count, last_rank, tail = len_ref[0], len_ref[1], len_ref[2]

    def finish(half_at, first):
        part_copy(half_at, 1).wait()
        part_copy(half_at, 2).wait()
        if first is None:
            first = part_ref[0, 0, 0:16, :].astype(jnp.float32)[0:1, :]
        index = lax.broadcasted_iota(jnp.int32, (part_len, dim), 0)
        rank = index // piece * 2 + half_at
        for part in range(head_count):
            rows = pl.ds(part * part_len, part_len)
            row = part * piece + index % piece
            live = (rank < live_count) & ((rank != last_rank) | (row < tail))
            keys = part_ref[half_at, 0, rows, :].astype(jnp.float32)
            part_ref[half_at, 0, rows, :] = jnp.where(live, keys, first).astype(jnp.bfloat16)
            values = part_ref[half_at, 1, rows, :].astype(jnp.float32)
            value_ref[half_at, rows, 0:dim] = jnp.where(live, values, 0.0).astype(jnp.bfloat16)
            value_ref[half_at, rows, dim:] = jnp.where(live, 1.0, 0.0).astype(jnp.bfloat16)
        return first

    sub = row_block // 2

    def prefix_rows(half_at, i):
        both = [
            pl.ds(pl.multiple_of(i * row_block + t * sub, sub), sub) for t in range(2)
        ]
        keys, values = part_ref[half_at, 0], value_ref[half_at]
        scores = [
            lax.dot_general(q_ref[rows, :], keys, (((1,), (1,)), ((), ())), preferred_element_type=jnp.float32)
            for rows in both
        ]
        for rows, s in zip(both, scores):
            m, acc = weigh(s, values, m_ref[rows, :], acc_ref[rows, :], scale)
            if half_at == 0:
                m_ref[rows, :] = m
                acc_ref[rows, :] = acc
            else:
                out_ref[rows, :] = (acc[:, :dim] / acc[:, dim:]).astype(out_ref.dtype)

    def keep_page(s):
        at = place_smem[0, s]
        cell = jnp.maximum(at - 1, 0)
        filled = jnp.full((piece, dim), at, jnp.int32) > 0
        for kv in range(2):
            page = fresh_in[cell // bound, cell % bound, kv].astype(jnp.float32)
            stored_ref[s, kv, mine, :] = jnp.where(filled, page, 0.0).astype(jnp.bfloat16)

    def stored_copy(which):
        part, peer = ((side, across), (side, by_pair), (across, by_pair))[which]
        rows = stored_ref.at[:, :, pl.ds(pl.multiple_of(part * piece, piece), piece), :]
        return remote(rows, rows, stored_send.at[which], stored_recv.at[which], "head", peer)

    def forward(half_at):
        part_copy(half_at, 0).wait()
        part_copy(half_at, 2).start()

    early = row_blocks * 3 // 4
    each(0, early, new_rows)
    collect(0)
    each(early, row_blocks, new_rows)
    forward(0)
    first = finish(0, None)
    each(0, row_blocks // 2, lambda i: prefix_rows(0, i))
    collect(1)
    each(row_blocks // 2, row_blocks * 7 // 8, lambda i: prefix_rows(0, i))
    forward(1)
    each(row_blocks * 7 // 8, row_blocks, lambda i: prefix_rows(0, i))
    finish(1, first)
    each(1, pools, lambda d: fresh_copy(d).wait())
    each(0, slots, keep_page)
    stored_copy(0).start()
    stored_copy(1).start()
    each(0, row_blocks // 2, lambda i: prefix_rows(1, i))
    stored_copy(0).wait()
    stored_copy(2).start()
    each(row_blocks // 2, row_blocks, lambda i: prefix_rows(1, i))
    stored_copy(1).wait()
    stored_copy(2).wait()


def fused(q, new_pairs, kv_pool, table, cells, source, length, slots, bucket, bound, pools, head_count, heads):
    rows, dim = q.shape
    new_pages, page_len = new_pairs.shape[1:3]
    piece = page_len // head_count
    max_pages = cells.shape[0]
    row_block = math.gcd(rows, 512)
    kernel = functools.partial(
        fused_kernel,
        scale=math.log2(math.e) / math.sqrt(dim),
        row_block=row_block,
        heads=heads,
    )
    bf16, dma = jnp.bfloat16, pltpu.SemaphoreType.DMA
    smem, vmem = pl.BlockSpec(memory_space=pltpu.SMEM), pl.BlockSpec(memory_space=pltpu.VMEM)
    half_len = max_pages // 2 * page_len
    return pl.pallas_call(
        kernel,
        out_shape=(
            jax.ShapeDtypeStruct((rows, dim), bf16),
            jax.ShapeDtypeStruct((slots, 2, page_len, dim), bf16),
        ),
        in_specs=[smem, smem, smem, vmem, vmem, vmem, pl.BlockSpec(memory_space=pl.ANY)],
        out_specs=(vmem, vmem),
        scratch_shapes=[
            pltpu.VMEM((kv_pool.shape[0], 2, piece, dim), bf16),
            pltpu.VMEM(table.shape, jnp.int32),
            pltpu.SMEM(table.shape, jnp.int32),
            pltpu.VMEM((1, 128), jnp.int32),
            pltpu.SMEM((1, 128), jnp.int32),
            pltpu.VMEM((2, pools, bucket // 2, 2, piece, dim), bf16),
            pltpu.VMEM((pools, bucket // 2, 2, piece, dim), bf16),
            pltpu.VMEM((pools, bucket // 2, 2, piece, dim), bf16),
            pltpu.VMEM((pools, bound, 2, piece, dim), bf16),
            pltpu.VMEM((pools, bound, 2, piece, dim), bf16),
            pltpu.VMEM((2, 2, half_len, dim), bf16),
            pltpu.VMEM((2, half_len, 2 * dim), bf16),
            pltpu.VMEM((new_pages * page_len, 2 * dim), bf16),
            pltpu.VMEM((rows, dim), jnp.float32),
            pltpu.VMEM((rows, 2 * dim), jnp.float32),
            dma,
            dma((2,)),
            dma((pools,)),
            dma((pools,)),
            dma((pools,)),
            dma((pools,)),
            dma((2, pools)),
            dma((2, pools)),
            dma((2, 3)),
            dma((2, 3)),
            dma((3,)),
            dma((3,)),
        ],
        compiler_params=pltpu.CompilerParams(
            vmem_limit_bytes=56 * 1024 * 1024, collective_id=0, has_side_effects=True
        ),
    )(length, cells, source, table, q, new_pairs, kv_pool)


def shards(queries, new_pairs, kv_pool, page_owner, page_slot, prefix_len, fresh_owner, fresh_slot):
    pool_count = lax.axis_size("pool")
    head_count = lax.axis_size("head")
    page_len = kv_pool.shape[2]
    dim = kv_pool.shape[3]
    max_pages = page_owner.shape[1]
    bucket = 2 * ((max_pages + pool_count - 1) // pool_count)
    new_len = new_pairs.shape[2]
    new_count = new_len // page_len
    write_bound = (new_count + pool_count - 1) // pool_count
    fresh_total = pool_count * write_bound
    length = prefix_len[0]

    live_pages = (length + page_len - 1) // page_len
    is_live = jnp.arange(max_pages, dtype=jnp.int32) < live_pages
    owners = page_owner[0]
    indices = jnp.arange(max_pages, dtype=jnp.int32)
    same_owner = owners[:, None] == owners[None, :]
    earlier = same_owner & (indices[:, None] > indices[None, :])
    ahead = earlier | (owners[:, None] > owners[None, :])
    position = jnp.sum(jnp.where(earlier & is_live[None, :], 1, 0), axis=1).astype(jnp.int32)
    rank = jnp.sum(jnp.where(ahead & is_live[None, :], 1, 0), axis=1).astype(jnp.int32)
    half_bucket = bucket // 2
    cell = owners * bucket + rank % 2 * half_bucket + position // 2
    cell = jnp.where(is_live, cell, -1)
    cell_at = jnp.arange(pool_count * bucket, dtype=jnp.int32)
    request_table = jnp.sum(
        jnp.where(cell[:, None] == cell_at[None, :], page_slot[0][:, None], 0), axis=0
    ).reshape(pool_count, bucket)
    order = jnp.where(is_live, rank % 2 * (max_pages // 2) + rank // 2, -1)
    half_cell = owners * half_bucket + position // 2
    cells = jnp.sum(jnp.where(order[:, None] == indices[None, :], half_cell[:, None], 0), axis=0)
    last_rank = jnp.sum(jnp.where(indices == live_pages - 1, rank, 0))
    lengths = jnp.stack([live_pages, last_rank, length - (live_pages - 1) * page_len]).astype(jnp.int32)
    fresh_cells, fresh_matches, _ = place_cells(
        fresh_owner[0],
        fresh_slot[0],
        jnp.ones((new_count,), dtype=bool),
        write_bound,
        pool_count,
    )
    source = jnp.sum(
        jnp.where(fresh_matches, jnp.arange(new_count, dtype=jnp.int32)[:, None], 0), axis=0
    )
    stamp = fresh_cells % write_bound + lax.axis_index("pool") * write_bound + 1
    spot = fresh_owner[0] * 128 + fresh_slot[0]
    lanes = jnp.arange(pool_count * 128, dtype=jnp.int32)
    places = jnp.sum(jnp.where(spot[:, None] == lanes[None, :], stamp[:, None], 0), axis=0)
    table = jnp.stack(
        [jnp.pad(request_table, ((0, 0), (0, 128 - bucket))), places.reshape(pool_count, 128)], axis=1
    )

    heads = queries.shape[2]
    attended, stored = fused(
        queries.reshape(-1, dim),
        new_pairs[0].reshape(2, new_count, page_len, dim),
        kv_pool,
        table,
        cells,
        source,
        lengths,
        fresh_total,
        bucket,
        write_bound,
        pool_count,
        head_count,
        heads,
    )
    return (attended.reshape(queries.shape), stored)


def solution(mesh):
    in_specs = (
        P("pool", None, "head", None),
        P("pool", None, None, None),
        P("pool", None, None, None),
        P("pool", None),
        P("pool", None),
        P("pool"),
        P("pool", None),
        P("pool", None),
    )
    out_specs = (P("pool", None, "head", None), P("pool", None, None, None))
    return jax.shard_map(shards, mesh=mesh, in_specs=in_specs, out_specs=out_specs, check_vma=False)
```

```python
import functools
import math

import jax
import jax.numpy as jnp
from jax import lax
from jax.experimental import pallas as pl
from jax.experimental.pallas import tpu as pltpu
from jax.sharding import PartitionSpec as P

masked_score = -1e30
MESH = pl.DeviceIdType.MESH


def place_cells(owners, slot_ids, is_live, per_owner, pool_count):
    how_many = owners.shape[0]
    indices = jnp.arange(how_many, dtype=jnp.int32)
    earlier = indices[:, None] > indices[None, :]
    same_owner = owners[:, None] == owners[None, :]
    position = jnp.sum(jnp.where(earlier & same_owner & is_live[None, :], 1, 0), axis=1).astype(
        jnp.int32
    )
    cell_ids = jnp.where(is_live, owners * per_owner + position, -1)
    matches = cell_ids[:, None] == jnp.arange(pool_count * per_owner, dtype=jnp.int32)[None, :]
    slot_table = jnp.sum(jnp.where(matches, slot_ids[:, None], 0), axis=0)
    return (cell_ids, matches, slot_table.reshape(pool_count, per_owner))


def absorb(q, k, v, m, acc, scale, keep=None):
    s = lax.dot_general(q, k, (((1,), (1,)), ((), ())), preferred_element_type=jnp.float32)
    if keep is not None:
        s = jnp.where(keep, s, masked_score)
    return weigh(s, v, m, acc, scale)


def weigh(s, v, m, acc, scale):
    top = jnp.max(s, axis=1, keepdims=True)
    new_m = jnp.maximum(m, top)
    p = jnp.exp2((s - new_m[:, :1]) * scale).astype(jnp.bfloat16)
    fade = jnp.exp2((m - new_m) * scale)[:, :1]
    acc = acc * fade + jnp.dot(p, v, preferred_element_type=jnp.float32)
    return new_m, acc


def fused_kernel(
    len_ref,
    cell_ref,
    source_ref,
    table_ref,
    q_ref,
    new_ref,
    pool_ref,
    out_ref,
    stored_ref,
    slice_ref,
    asked_ref,
    asked_smem,
    place_ref,
    place_smem,
    page_out,
    first_in,
    second_in,
    fresh_out,
    fresh_in,
    part_ref,
    value_ref,
    new_value_ref,
    m_ref,
    acc_ref,
    load_sem,
    small_sem,
    table_send,
    table_recv,
    fresh_send,
    fresh_recv,
    page_send,
    page_recv,
    part_send,
    part_recv,
    stored_send,
    stored_recv,
    *,
    scale,
    row_block,
    heads,
):
    _, pools, bucket, _, piece, dim = page_out.shape
    part_len = cell_ref.shape[0] // 2 * piece
    head_count = part_ref.shape[2] // part_len
    bound = fresh_out.shape[1]
    slots = stored_ref.shape[0]
    page_len = stored_ref.shape[2]
    max_pages = cell_ref.shape[0]
    new_pages = new_ref.shape[1]
    page_in = (first_in, second_in)
    me = lax.axis_index("pool")
    side = lax.axis_index("head")
    mine = pl.ds(pl.multiple_of(side * piece, piece), piece)
    by_pair = side + 1 - 2 * (side % 2)
    half = head_count // 2
    across = (side + half) % head_count

    load = pltpu.make_async_copy(pool_ref.at[:, :, mine, :], slice_ref, load_sem)
    load.start()

    barrier = pltpu.get_barrier_semaphore()

    def greet(d, carry):
        pl.semaphore_signal(barrier, inc=1, device_id={"pool": (me + d) % pools}, device_id_type=MESH)
        return carry

    lax.fori_loop(1, pools, greet, 0)
    for peer in (by_pair, across):
        pl.semaphore_signal(barrier, inc=1, device_id={"head": peer}, device_id_type=MESH)
    pl.semaphore_wait(barrier, pools - 1 + 2)

    def remote(src, dst, send, recv, axis, peer):
        return pltpu.make_async_remote_copy(
            src_ref=src,
            dst_ref=dst,
            send_sem=send,
            recv_sem=recv,
            device_id={axis: peer},
            device_id_type=MESH,
        )

    def table_copy(d):
        to = (me + d) % pools
        return remote(table_ref.at[to], asked_ref.at[me], table_send.at[d], table_recv.at[d], "pool", to)

    def fresh_copy(d):
        to = (me + d) % pools
        return remote(fresh_out.at[to], fresh_in.at[me], fresh_send.at[d], fresh_recv.at[d], "pool", to)

    def page_copy(kv, d):
        to = (me + d) % pools
        return remote(
            page_out.at[kv, to], page_in[kv].at[me], page_send.at[kv, d], page_recv.at[kv, d], "pool", to
        )

    def each(start, stop, act):
        def body(d, carry):
            act(d)
            return carry

        lax.fori_loop(start, stop, body, 0)

    each(1, pools, lambda d: table_copy(d).start())
    asked_ref[me] = table_ref[me]
    load.wait()
    each(1, pools, lambda d: table_copy(d).wait())
    total = asked_ref[0, 1:2, :]
    for r in range(1, pools):
        total = total + asked_ref[r, 1:2, :]
    place_ref[...] = total
    to_smem = pltpu.make_async_copy(asked_ref, asked_smem, small_sem.at[0])
    to_smem.start()
    place_copy = pltpu.make_async_copy(place_ref, place_smem, small_sem.at[1])
    place_copy.start()
    to_smem.wait()
    place_copy.wait()

    def pages_to(part, d):
        to = (me + d) % pools
        for c in range(bucket):
            page_out[part, to, c] = slice_ref[asked_smem[to, 0, part * bucket + c]]

    def send_half(part):
        def send_pages(d):
            pages_to(part, d)
            page_copy(part, d).start()

        each(1, pools, send_pages)
        pages_to(part, 0)
        page_in[part][me] = page_out[part, me]

    send_half(0)

    def fresh_to(d):
        to = (me + d) % pools
        for c in range(bound):
            page = source_ref[to * bound + c]
            for kv in range(2):
                fresh_out[to, c, kv] = new_ref[kv, page, mine, :]

    def send_fresh(d):
        fresh_to(d)
        fresh_copy(d).start()

    new_value_ref[:, 0:dim] = new_ref[1].reshape(new_pages * page_len, dim)
    new_value_ref[:, dim:] = jnp.ones((new_pages * page_len, dim), jnp.bfloat16)
    tokens = row_block // heads
    row_blocks = q_ref.shape[0] // row_block

    def new_rows(i):
        rows = pl.ds(pl.multiple_of(i * row_block, row_block), row_block)
        q = q_ref[rows, :]
        m = jnp.full((row_block, dim), masked_score, jnp.float32)
        acc = jnp.zeros((row_block, 2 * dim), jnp.float32)

        def new_block(at, carry, keep=None):
            k = new_ref[0, pl.ds(at * (tokens // page_len), tokens // page_len)].reshape(tokens, dim)
            v = new_value_ref[pl.ds(pl.multiple_of(at * tokens, tokens), tokens), :]
            return absorb(q, k, v, *carry, scale, keep)

        row_token = lax.broadcasted_iota(jnp.int32, (row_block, tokens), 0) // heads
        keep = lax.broadcasted_iota(jnp.int32, (row_block, tokens), 1) <= row_token
        m, acc = lax.fori_loop(0, i, new_block, new_block(i, (m, acc), keep))
        m_ref[rows, :] = m
        acc_ref[rows, :] = acc

    def part_rows(part):
        return pl.ds(pl.multiple_of(part * part_len, part_len), part_len)

    def part_copy(half_at, which):
        part, peer = ((side, across), (side, by_pair), (across, by_pair))[which]
        return remote(
            part_ref.at[half_at, :, part_rows(part), :],
            part_ref.at[half_at, :, part_rows(part), :],
            part_send.at[half_at, which],
            part_recv.at[half_at, which],
            "head",
            peer,
        )

    def collect(half_at):
        each(1, pools, lambda d: page_copy(half_at, d).wait())
        count = part_len // piece

        def four(g):
            for j in range(4):
                cell = cell_ref[half_at * count + g * 4 + j]
                rows = pl.ds(pl.multiple_of(side * part_len + (g * 4 + j) * piece, piece), piece)
                for kv in range(2):
                    part_ref[half_at, kv, rows, :] = page_in[half_at][cell // bucket, cell % bucket, kv]

        each(0, count // 4, four)
        part_copy(half_at, 0).start()
        part_copy(half_at, 1).start()

    live_count, last_rank, tail = len_ref[0], len_ref[1], len_ref[2]

    def finish(half_at, first):
        part_copy(half_at, 1).wait()
        part_copy(half_at, 2).wait()
        if first is None:
            first = part_ref[0, 0, 0:16, :].astype(jnp.float32)[0:1, :]
        index = lax.broadcasted_iota(jnp.int32, (part_len, dim), 0)
        rank = index // piece * 2 + half_at
        for part in range(head_count):
            rows = pl.ds(part * part_len, part_len)
            row = part * piece + index % piece
            live = (rank < live_count) & ((rank != last_rank) | (row < tail))
            keys = part_ref[half_at, 0, rows, :].astype(jnp.float32)
            part_ref[half_at, 0, rows, :] = jnp.where(live, keys, first).astype(jnp.bfloat16)
            values = part_ref[half_at, 1, rows, :].astype(jnp.float32)
            value_ref[half_at, rows, 0:dim] = jnp.where(live, values, 0.0).astype(jnp.bfloat16)
            value_ref[half_at, rows, dim:] = jnp.where(live, 1.0, 0.0).astype(jnp.bfloat16)
        return first

    sub = row_block // 2

    def prefix_rows(half_at, i):
        both = [
            pl.ds(pl.multiple_of(i * row_block + t * sub, sub), sub) for t in range(2)
        ]
        keys, values = part_ref[half_at, 0], value_ref[half_at]
        scores = [
            lax.dot_general(q_ref[rows, :], keys, (((1,), (1,)), ((), ())), preferred_element_type=jnp.float32)
            for rows in both
        ]
        for rows, s in zip(both, scores):
            m, acc = weigh(s, values, m_ref[rows, :], acc_ref[rows, :], scale)
            if half_at == 0:
                m_ref[rows, :] = m
                acc_ref[rows, :] = acc
            else:
                out_ref[rows, :] = (acc[:, :dim] / acc[:, dim:]).astype(out_ref.dtype)

    def keep_page(s):
        at = place_smem[0, s]
        cell = jnp.maximum(at - 1, 0)
        filled = jnp.full((piece, dim), at, jnp.int32) > 0
        for kv in range(2):
            page = fresh_in[cell // bound, cell % bound, kv].astype(jnp.float32)
            stored_ref[s, kv, mine, :] = jnp.where(filled, page, 0.0).astype(jnp.bfloat16)

    def stored_copy(which):
        part, peer = ((side, across), (side, by_pair), (across, by_pair))[which]
        rows = stored_ref.at[:, :, pl.ds(pl.multiple_of(part * piece, piece), piece), :]
        return remote(rows, rows, stored_send.at[which], stored_recv.at[which], "head", peer)

    def forward(half_at):
        part_copy(half_at, 0).wait()
        part_copy(half_at, 2).start()

    early = row_blocks * 3 // 4
    each(0, row_blocks // 2, new_rows)
    send_half(1)
    each(row_blocks // 2, early, new_rows)
    collect(0)
    each(1, pools, send_fresh)
    fresh_to(0)
    fresh_in[me] = fresh_out[me]
    each(early, row_blocks - 1, new_rows)
    forward(0)
    each(row_blocks - 1, row_blocks, new_rows)
    first = finish(0, None)
    each(0, row_blocks // 2, lambda i: prefix_rows(0, i))
    collect(1)
    each(row_blocks // 2, row_blocks * 7 // 8, lambda i: prefix_rows(0, i))
    forward(1)
    each(row_blocks * 7 // 8, row_blocks, lambda i: prefix_rows(0, i))
    finish(1, first)
    each(1, pools, lambda d: fresh_copy(d).wait())
    each(0, slots, keep_page)
    stored_copy(0).start()
    stored_copy(1).start()
    each(0, row_blocks // 2, lambda i: prefix_rows(1, i))
    stored_copy(0).wait()
    stored_copy(2).start()
    each(row_blocks // 2, row_blocks, lambda i: prefix_rows(1, i))
    stored_copy(1).wait()
    stored_copy(2).wait()


def fused(q, new_pairs, kv_pool, table, cells, source, length, slots, bucket, bound, pools, head_count, heads):
    rows, dim = q.shape
    new_pages, page_len = new_pairs.shape[1:3]
    piece = page_len // head_count
    max_pages = cells.shape[0]
    row_block = math.gcd(rows, 512)
    kernel = functools.partial(
        fused_kernel,
        scale=math.log2(math.e) / math.sqrt(dim),
        row_block=row_block,
        heads=heads,
    )
    bf16, dma = jnp.bfloat16, pltpu.SemaphoreType.DMA
    smem, vmem = pl.BlockSpec(memory_space=pltpu.SMEM), pl.BlockSpec(memory_space=pltpu.VMEM)
    half_len = max_pages // 2 * page_len
    return pl.pallas_call(
        kernel,
        out_shape=(
            jax.ShapeDtypeStruct((rows, dim), bf16),
            jax.ShapeDtypeStruct((slots, 2, page_len, dim), bf16),
        ),
        in_specs=[smem, smem, smem, vmem, vmem, vmem, pl.BlockSpec(memory_space=pl.ANY)],
        out_specs=(vmem, vmem),
        scratch_shapes=[
            pltpu.VMEM((kv_pool.shape[0], 2, piece, dim), bf16),
            pltpu.VMEM(table.shape, jnp.int32),
            pltpu.SMEM(table.shape, jnp.int32),
            pltpu.VMEM((1, 128), jnp.int32),
            pltpu.SMEM((1, 128), jnp.int32),
            pltpu.VMEM((2, pools, bucket // 2, 2, piece, dim), bf16),
            pltpu.VMEM((pools, bucket // 2, 2, piece, dim), bf16),
            pltpu.VMEM((pools, bucket // 2, 2, piece, dim), bf16),
            pltpu.VMEM((pools, bound, 2, piece, dim), bf16),
            pltpu.VMEM((pools, bound, 2, piece, dim), bf16),
            pltpu.VMEM((2, 2, half_len, dim), bf16),
            pltpu.VMEM((2, half_len, 2 * dim), bf16),
            pltpu.VMEM((new_pages * page_len, 2 * dim), bf16),
            pltpu.VMEM((rows, dim), jnp.float32),
            pltpu.VMEM((rows, 2 * dim), jnp.float32),
            dma,
            dma((2,)),
            dma((pools,)),
            dma((pools,)),
            dma((pools,)),
            dma((pools,)),
            dma((2, pools)),
            dma((2, pools)),
            dma((2, 3)),
            dma((2, 3)),
            dma((3,)),
            dma((3,)),
        ],
        compiler_params=pltpu.CompilerParams(
            vmem_limit_bytes=56 * 1024 * 1024, collective_id=0, has_side_effects=True
        ),
    )(length, cells, source, table, q, new_pairs, kv_pool)


def shards(queries, new_pairs, kv_pool, page_owner, page_slot, prefix_len, fresh_owner, fresh_slot):
    pool_count = lax.axis_size("pool")
    head_count = lax.axis_size("head")
    page_len = kv_pool.shape[2]
    dim = kv_pool.shape[3]
    max_pages = page_owner.shape[1]
    bucket = 2 * ((max_pages + pool_count - 1) // pool_count)
    new_len = new_pairs.shape[2]
    new_count = new_len // page_len
    write_bound = (new_count + pool_count - 1) // pool_count
    fresh_total = pool_count * write_bound
    length = prefix_len[0]

    live_pages = (length + page_len - 1) // page_len
    is_live = jnp.arange(max_pages, dtype=jnp.int32) < live_pages
    owners = page_owner[0]
    indices = jnp.arange(max_pages, dtype=jnp.int32)
    same_owner = owners[:, None] == owners[None, :]
    earlier = same_owner & (indices[:, None] > indices[None, :])
    ahead = earlier | (owners[:, None] > owners[None, :])
    position = jnp.sum(jnp.where(earlier & is_live[None, :], 1, 0), axis=1).astype(jnp.int32)
    rank = jnp.sum(jnp.where(ahead & is_live[None, :], 1, 0), axis=1).astype(jnp.int32)
    half_bucket = bucket // 2
    cell = owners * bucket + rank % 2 * half_bucket + position // 2
    cell = jnp.where(is_live, cell, -1)
    cell_at = jnp.arange(pool_count * bucket, dtype=jnp.int32)
    request_table = jnp.sum(
        jnp.where(cell[:, None] == cell_at[None, :], page_slot[0][:, None], 0), axis=0
    ).reshape(pool_count, bucket)
    order = jnp.where(is_live, rank % 2 * (max_pages // 2) + rank // 2, -1)
    half_cell = owners * half_bucket + position // 2
    cells = jnp.sum(jnp.where(order[:, None] == indices[None, :], half_cell[:, None], 0), axis=0)
    last_rank = jnp.sum(jnp.where(indices == live_pages - 1, rank, 0))
    lengths = jnp.stack([live_pages, last_rank, length - (live_pages - 1) * page_len]).astype(jnp.int32)
    fresh_cells, fresh_matches, _ = place_cells(
        fresh_owner[0],
        fresh_slot[0],
        jnp.ones((new_count,), dtype=bool),
        write_bound,
        pool_count,
    )
    source = jnp.sum(
        jnp.where(fresh_matches, jnp.arange(new_count, dtype=jnp.int32)[:, None], 0), axis=0
    )
    stamp = fresh_cells % write_bound + lax.axis_index("pool") * write_bound + 1
    spot = fresh_owner[0] * 128 + fresh_slot[0]
    lanes = jnp.arange(pool_count * 128, dtype=jnp.int32)
    places = jnp.sum(jnp.where(spot[:, None] == lanes[None, :], stamp[:, None], 0), axis=0)
    table = jnp.stack(
        [jnp.pad(request_table, ((0, 0), (0, 128 - bucket))), places.reshape(pool_count, 128)], axis=1
    )

    heads = queries.shape[2]
    attended, stored = fused(
        queries.reshape(-1, dim),
        new_pairs[0].reshape(2, new_count, page_len, dim),
        kv_pool,
        table,
        cells,
        source,
        lengths,
        fresh_total,
        bucket,
        write_bound,
        pool_count,
        head_count,
        heads,
    )
    return (attended.reshape(queries.shape), stored)


def solution(mesh):
    in_specs = (
        P("pool", None, "head", None),
        P("pool", None, None, None),
        P("pool", None, None, None),
        P("pool", None),
        P("pool", None),
        P("pool"),
        P("pool", None),
        P("pool", None),
    )
    out_specs = (P("pool", None, "head", None), P("pool", None, None, None))
    return jax.shard_map(shards, mesh=mesh, in_specs=in_specs, out_specs=out_specs, check_vma=False)
```
